128 devices in a mesh: rows: 128 (over x, z, y, core).
Axes of the slice: x: 4, y: 4, z: 4, core: 2. Of those that a mesh axis runs over, the one named last changes fastest.
Arguments:
- seeds: int32 [512], P('rows'), may hold values from 0 to 16777215
- offset: int32 [1], replicated, may hold values from 0 to 64512
Outputs:
- field_real: float32 [32768, 1024], P('rows')
- field_imag: float32 [32768, 1024], P('rows')
The draws below stay inside these ranges and needn't reach their ends.
All inputs are finite; a program needn't handle non-finite values.
Results may differ from the reference program's by a relative error of at most 0.00013.
Values sent between devices are 32-bit elements; how exact they have to be, the bound alone decides.
A program may use at most 64 MiB of HBM per device.

```python
import math
import jax
import jax.numpy as jnp

NY = 32768
NXG = 65536
STRIP = 1024
KAPPA = 8192
SEED_BLOCK = 64
NSEED = 512


def plant(entries, key, low, top_value):
    extent = entries.shape
    index_at = [jax.random.randint(jax.random.fold_in(key, axis), (), 0, extent[axis]) for axis in range(len(extent))]
    entries = entries.at[tuple(index_at)].set(low)
    longest = extent.index(max(extent))
    index_at[longest] = (index_at[longest] + 1) % extent[longest]
    return entries.at[tuple(index_at)].set(top_value)


def setup_inputs(seed: int = 0) -> dict:
    key_list = jax.random.split(jax.random.key(seed), 3)
    return {
        "seeds": plant(jax.random.randint(key_list[0], (NSEED,), 0, 16777216), jax.random.fold_in(key_list[0], 1), 0, 16777215).astype(jnp.int32),
        "offset": jax.random.randint(key_list[1], (1,), 0, NXG - STRIP + 1).astype(jnp.int32),
    }


def uniform_noise(seed_grid, wave_grid, column_grid, salt):
    h = (seed_grid % 65521 + wave_grid * 7919 % 65521 + column_grid * 30011 % 65521 + salt) % 65521
    h = (h % 46337 * (h % 46337) + column_grid % 4099 * 7 + salt) % 65521
    h = (h * 32719 + wave_grid % 8191 * 13) % 65521
    h = (h % 46337 * (h % 46337) + seed_grid % 32749) % 65521
    unit = (h.astype(jnp.float32) + 0.5) / 65521.0
    return 3.4641016151377544 * (unit - 0.5)

def spectrum(seed_rows, waves, offset):
    column = offset[0] + jnp.arange(STRIP, dtype=jnp.int32)
    wave_x = jnp.minimum(column, NXG - column).astype(jnp.float32)
    wave_y = jnp.minimum(waves, NY - waves).astype(jnp.float32)
    radius = (wave_x[None, :] * wave_x[None, :] + wave_y[:, None] * wave_y[:, None]) / (float(KAPPA) * float(KAPPA))
    amplitude = 2.0 * (1.0 + radius) ** (-0.75)
    seed_grid = seed_rows[:, None]
    wave_grid = waves[:, None]
    column_grid = column[None, :]
    noise_real = uniform_noise(seed_grid, wave_grid, column_grid, 17)
    noise_imag = uniform_noise(seed_grid, wave_grid, column_grid, 29011)
    return (amplitude * noise_real, amplitude * noise_imag)

def reference(seeds, offset):
    waves = jnp.arange(NY, dtype=jnp.int32)
    seed_rows = seeds[waves // SEED_BLOCK]
    real_part, imag_part = spectrum(seed_rows, waves, offset)
    field = jnp.fft.ifft(real_part + 1j * imag_part, axis=0) * math.sqrt(NY)
    return (jnp.real(field).astype(jnp.float32), jnp.imag(field).astype(jnp.float32))
```

```python
import itertools
import math
import random

import jax
import jax.numpy as jnp
import ml_dtypes
import numpy as np
from jax import lax
from jax.experimental import pallas as pl
from jax.experimental.pallas import tpu as pltpu
from jax.sharding import PartitionSpec as P

NY = 32768
NXG = 65536
STRIP = 1024
KAPPA = 8192
N = 128
DEPTH = 256
PAIRS = 64
COLS = STRIP // PAIRS
NC = 4
CHUNKS = COLS // NC
Q = 2 * COLS
MOD = 65521
MESH = pl.DeviceIdType.MESH
F32 = jnp.float32
BF16 = jnp.bfloat16


def hops(offset):
    return sum((0, 1, 2, 1)[a] for a in offset[:3])


def is_near(offset):
    if hops(offset) != 3:
        return hops(offset) < 3
    if 2 not in offset[:3]:
        return sum(a == 3 for a in offset[:3]) % 2 == 0
    return (offset.index(0) + 1) % 3 == offset[:3].index(2)


def near_offsets():
    every = itertools.product(range(4), range(4), range(4), range(2))
    near = [offset for offset in every if is_near(offset)]
    random.Random(3).shuffle(near)
    return near


NEAR = near_offsets()


def tables():
    k1 = np.arange(N)[:, None]
    k2 = np.arange(DEPTH)[None, :]
    k = k1 + N * k2
    wave_hash = ((7919 * k) % MOD).astype(np.int32)
    wave_add = (13 * (k % 8191) + 16000 * MOD).astype(np.int32)
    ky = np.minimum(k, NY - k) / KAPPA
    wave_sq = (1.0 + ky * ky).astype(np.float32)
    angle = 2.0 * np.pi * (k1 * k2) / NY
    twist = np.stack([np.cos(angle), np.sin(angle)]).astype(np.float32)
    i = np.arange(DEPTH)
    angle = 2.0 * np.pi * (i[:, None] * i[None, :] % DEPTH) / DEPTH
    c, s = np.cos(angle), np.sin(angle)
    inner = np.block([[c, s], [-s, c]]).astype(np.float32)
    inner_hi = inner.astype(ml_dtypes.bfloat16)
    inner_lo = (inner - inner_hi.astype(np.float32)).astype(ml_dtypes.bfloat16)
    masks = [((a * 4 + b) * 4 + c) * 2 + d for a, b, c, d in NEAR]
    masks = np.broadcast_to(np.array(masks, np.int32)[:, None], (PAIRS, N))
    return (
        np.stack([wave_hash, wave_add]),
        wave_sq,
        twist,
        np.stack([inner_hi, inner_lo]),
        np.ascontiguousarray(masks),
    )


def split(x):
    hi = x.astype(BF16)
    return hi, (x - hi.astype(F32)).astype(BF16)


def mod_small(s, m):
    q = (s.astype(F32) * np.float32(1.0 / m)).astype(jnp.int32)
    r = s - q * m
    r = jnp.where(r < 0, r + m, r)
    return jnp.where(r >= m, r - m, r)


def noise(base, c1, c2, wave_add, seed_add):
    inv = np.float32(1.0 / MOD)
    t = base + c1
    t = jnp.where(t >= MOD, t - MOD, t)
    u = jnp.where(t >= 46337, t - 46337, t)
    p = u * u
    w = (p >> 16) * 32138 - (p & 0xFFFF) * 32802 + (wave_add + c2)
    w = w - (w >> 16) * MOD
    f = w.astype(F32)
    h = f - jnp.floor(f * inv + np.float32(0.5) * inv) * np.float32(MOD)
    u = jnp.where(h >= 46337.0, h - 46337.0, h).astype(jnp.int32)
    p = u * u + seed_add
    v = p - (p >> 16) * MOD
    x = v.astype(F32) * inv + np.float32(0.5 / MOD - 0.5)
    return x - jnp.round(x)


def xor_values(a):
    return [a, a + 1 - 2 * (a % 2), (a + 2) % 4, 3 - a]


def synth(
    offset, seeds, ints_hbm, wave_sq_hbm, twist_hbm, inner_hbm, masks_hbm, out,
    ints, seed2, wave_sq, twist, inner, masks, amp, xhi, xlo, ybuf, zbuf, outer,
    seed_row, seed_all, seeds_out, par, parf, tsem, gsem, grecv, ssem, rsem,
):
    me = lax.axis_index("rows")
    mx, mz, my, mc = me // 32, me // 8 % 4, me // 2 % 4, me % 2
    barrier = pltpu.get_barrier_semaphore()

    def greet(i, _):
        pl.semaphore_signal(barrier, inc=1, device_id=(lax.rem(me + i, N),), device_id_type=MESH)
        return 0

    lax.fori_loop(1, N, greet, 0)

    loads = [
        pltpu.make_async_copy(a, b, tsem.at[i])
        for i, (a, b) in enumerate(
            [(wave_sq_hbm, wave_sq), (masks_hbm, masks), (ints_hbm, ints), (inner_hbm, inner), (twist_hbm, twist)]
        )
    ]
    for load in loads:
        load.start()

    upper = mx // 2
    flip = lambda a: (a + 2 * upper) % 4
    pair = (mx % 2) * 32 + flip(mz) * 8 + flip(my) * 2 + mc

    lane = lax.broadcasted_iota(jnp.int32, (8, N), 1)
    odd, half = lane % 2, lane // 2 % 2
    seed_row[...] = jnp.where(
        half == 0, jnp.where(odd == 0, seeds[0], seeds[2]), jnp.where(odd == 0, seeds[1], seeds[3])
    )

    for j in range(COLS):
        g = offset[0] + (j * PAIRS + pair)
        c = g * 30011 % MOD
        d = g % 4099 * 7
        par[j, 0] = (c + 17) % MOD
        par[j, 1] = (c + 29011) % MOD
        par[j, 2] = (d + 17) * 32719 % MOD
        par[j, 3] = (d + 29011) * 32719 % MOD
        kx = jnp.minimum(g, NXG - g).astype(F32) * np.float32(1.0 / KAPPA)
        parf[j] = kx * kx

    loads[0].wait()
    loads[1].wait()
    dest = lax.bitwise_xor(masks[...], me)
    k1 = lax.broadcasted_iota(jnp.int32, (PAIRS, N), 1)
    angle = (dest * k1 % N).astype(F32) * np.float32(2.0 * math.pi / N)
    c, s = jnp.cos(angle), jnp.sin(angle)
    for x, i, k in ((c, 0, 0), (-s, 0, 1), (s, 1, 0), (c, 1, 1)):
        hi, lo = split(x)
        rows, cols = pl.ds(PAIRS * i, PAIRS), pl.ds(N * k, N)
        outer[0, rows, cols] = hi
        outer[1, rows, cols] = lo

    scale = np.float32(2.0 * 3.4641016151377544 / math.sqrt(NY))

    def amplitude(i, _):
        rows = pl.ds(pl.multiple_of(i * 16, 16), 16)
        z0 = wave_sq[rows]
        for j in range(COLS):
            y = lax.rsqrt(z0 + parf[j])
            amp[j, rows] = y * y * lax.rsqrt(y) * scale
        return 0

    lax.fori_loop(0, N // 16, amplitude, 0)

    for load in loads[2:]:
        load.wait()

    pl.semaphore_wait(barrier, N - 1)

    pltpu.make_async_copy(seed_row.at[0], seed_all.at[me], grecv).start()

    def seed_copy(i):
        return pltpu.make_async_remote_copy(
            src_ref=seed_row.at[0],
            dst_ref=seed_all.at[me],
            send_sem=gsem,
            recv_sem=grecv,
            device_id=(lax.rem(me + i, N),),
            device_id_type=MESH,
        )

    def send_seeds(i, _):
        seed_copy(i).start()
        return 0

    lax.fori_loop(1, N, send_seeds, 0)
    pltpu.make_async_copy(seed_all, seed_all, grecv).wait()

    got = seed_all[...]
    turned = pltpu.roll(got, 2, 1)
    lane = lax.broadcasted_iota(jnp.int32, (N, N), 1)
    row = lax.broadcasted_iota(jnp.int32, (N, N), 0)
    mine = lane // 2 == row % 64
    for h in range(2):
        picked = jnp.where(mine, jnp.where(lane // 2 % 2 == h, got, turned), 0).astype(F32)
        for t in range(2):
            s = jnp.sum(picked[64 * t : 64 * t + 64], axis=0, keepdims=True).astype(jnp.int32)
            rows, cols = pl.ds(64 * h, 64), pl.ds(128 * t, 128)
            a = ints[0, rows, cols] + jnp.broadcast_to(mod_small(s, MOD), (64, 128))
            ints[0, rows, cols] = jnp.where(a >= MOD, a - MOD, a)
            seed2[rows, cols] = jnp.broadcast_to(mod_small(s, 32749), (64, 128))

    xs, zs = [v * 32 for v in xor_values(mx)], [v * 8 for v in xor_values(mz)]
    ys, cs = [v * 2 for v in xor_values(my)], [mc, 1 - mc]

    def chunk(ch, _):
        for jj in range(NC):
            j = ch * NC + jj

            def block(i, _):
                at = pl.multiple_of(i * 16, 16)
                rows = pl.ds(at, 16)
                base, wave_add, seed_add = ints[0, rows], ints[1, rows], seed2[rows]
                a = amp[j, rows]
                for part in range(2):
                    f = a * noise(base, par[j, part], par[j, 2 + part], wave_add, seed_add)
                    hi, lo = split(f)
                    to = pl.ds(jj * N + at, 16)
                    xhi[to, part * DEPTH : (part + 1) * DEPTH] = hi
                    xlo[to, part * DEPTH : (part + 1) * DEPTH] = lo
                return 0

            lax.fori_loop(0, N // 16, block, 0, unroll=2)
        dot = lambda a, b: jnp.dot(a, b, preferred_element_type=F32)
        ybuf[...] = dot(xhi[...], inner[0]) + dot(xlo[...], inner[0]) + dot(xhi[...], inner[1])
        for jj in range(NC):
            yr, yi = ybuf[jj * N : (jj + 1) * N, :DEPTH], ybuf[jj * N : (jj + 1) * N, DEPTH:]
            tc, ts = twist[0], twist[1]
            hi, lo = split(jnp.concatenate([yr * tc - yi * ts, yr * ts + yi * tc], axis=0))
            z = dot(outer[0], hi) + dot(outer[0], lo) + dot(outer[1], hi)
            q = (ch * NC + jj) * 2
            zbuf[q] = z[:PAIRS]
            zbuf[q + 1] = z[PAIRS:]
        qs = pl.ds(ch * (2 * NC), 2 * NC)
        for t, (a, b, c, d) in enumerate(NEAR):
            if (a, b, c, d) == (0, 0, 0, 0):
                pltpu.make_async_copy(zbuf.at[qs, t], out.at[qs, pair], rsem.at[ch]).start()
            else:
                pltpu.make_async_remote_copy(
                    src_ref=zbuf.at[qs, t],
                    dst_ref=out.at[qs, pair],
                    send_sem=ssem.at[ch],
                    recv_sem=rsem.at[ch],
                    device_id=(xs[a] + zs[b] + ys[c] + cs[d],),
                    device_id_type=MESH,
                ).start()
        return 0

    lax.fori_loop(0, CHUNKS, chunk, 0)

    pltpu.make_async_copy(seeds_out, seeds_out, gsem).wait()
    for ch in range(CHUNKS):
        qs = pl.ds(ch * 2 * NC, 2 * NC)
        pltpu.make_async_copy(out.at[qs], out.at[qs], rsem.at[ch]).wait()
        sent = amp.at[pl.ds(0, 9), pl.ds(0, (PAIRS - 1) * 2 * NC // 9)]
        pltpu.make_async_copy(sent, sent, ssem.at[ch]).wait()


def turn(block, real, imag):
    for c, to in ((0, real), (1, imag)):
        to[...] = jnp.concatenate([block[c], block[2 + c]], axis=0).T


def shards(seeds, offset):
    ints, wave_sq, twist, inner, masks = tables()
    anywhere = pl.BlockSpec(memory_space=pl.ANY)
    scalar = pl.BlockSpec(memory_space=pltpu.SMEM)
    dma = pltpu.SemaphoreType.DMA
    blocks = pl.pallas_call(
        synth,
        out_shape=jax.ShapeDtypeStruct((Q, PAIRS, DEPTH), F32),
        in_specs=[scalar, scalar] + [anywhere] * 5,
        out_specs=anywhere,
        scratch_shapes=[
            pltpu.VMEM((2, N, DEPTH), jnp.int32),
            pltpu.VMEM((N, DEPTH), jnp.int32),
            pltpu.VMEM((N, DEPTH), F32),
            pltpu.VMEM((2, N, DEPTH), F32),
            pltpu.VMEM((2, 2 * DEPTH, 2 * DEPTH), BF16),
            pltpu.VMEM((PAIRS, N), jnp.int32),
            pltpu.VMEM((COLS, N, DEPTH), F32),
            pltpu.VMEM((NC * N, 2 * DEPTH), BF16),
            pltpu.VMEM((NC * N, 2 * DEPTH), BF16),
            pltpu.VMEM((NC * N, 2 * DEPTH), F32),
            pltpu.VMEM((Q, PAIRS, DEPTH), F32),
            pltpu.VMEM((2, 2 * PAIRS, 2 * N), BF16),
            pltpu.VMEM((8, N), jnp.int32),
            pltpu.VMEM((N, N), jnp.int32),
            pltpu.VMEM((N - 1, 1, N), jnp.int32),
            pltpu.SMEM((COLS, 4), jnp.int32),
            pltpu.SMEM((COLS,), F32),
            dma((5,)),
            dma,
            dma,
            dma((CHUNKS,)),
            dma((CHUNKS,)),
        ],
        compiler_params=pltpu.CompilerParams(
            collective_id=0, has_side_effects=True, vmem_limit_bytes=48 * 2**20
        ),
    )(offset, seeds, ints, wave_sq, twist, inner, masks)
    out = pl.BlockSpec((DEPTH, N), lambda i: (0, i))
    return pl.pallas_call(
        turn,
        grid=(STRIP // N,),
        out_shape=[jax.ShapeDtypeStruct((DEPTH, STRIP), F32)] * 2,
        in_specs=[pl.BlockSpec((4, PAIRS, DEPTH), lambda i: (i, 0, 0))],
        out_specs=[out, out],
    )(blocks)


def solution(mesh):
    in_specs = (P("rows"), P())
    out_specs = (P("rows", None), P("rows", None))
    return jax.shard_map(shards, mesh=mesh, in_specs=in_specs, out_specs=out_specs, check_vma=False)
```

```python
import itertools
import math
import random

import jax
import jax.numpy as jnp
import numpy as np
from jax import lax
from jax.experimental import pallas as pl
from jax.experimental.pallas import tpu as pltpu
from jax.sharding import PartitionSpec as P

NY = 32768
NXG = 65536
STRIP = 1024
KAPPA = 8192
N = 128
DEPTH = 256
PAIRS = 64
COLS = STRIP // PAIRS
NC = 4
CHUNKS = COLS // NC
Q = 2 * COLS
MOD = 65521
MESH = pl.DeviceIdType.MESH
F32 = jnp.float32
BF16 = jnp.bfloat16


def hops(offset):
    return sum((0, 1, 2, 1)[a] for a in offset[:3])


def is_near(offset):
    if hops(offset) != 3:
        return hops(offset) < 3
    if 2 not in offset[:3]:
        return sum(a == 3 for a in offset[:3]) % 2 == 0
    return (offset.index(0) + 1) % 3 == offset[:3].index(2)


def near_offsets():
    every = itertools.product(range(4), range(4), range(4), range(2))
    near = [offset for offset in every if is_near(offset)]
    random.Random(3).shuffle(near)
    return near


NEAR = near_offsets()


MASKS = [((a * 4 + b) * 4 + c) * 2 + d for a, b, c, d in NEAR]


def split(x):
    hi = x.astype(BF16)
    return hi, (x - hi.astype(F32)).astype(BF16)


def mod_small(s, m):
    q = (s.astype(F32) * np.float32(1.0 / m)).astype(jnp.int32)
    r = s - q * m
    r = jnp.where(r < 0, r + m, r)
    return jnp.where(r >= m, r - m, r)


def noise(base, c1, c2, wave_add, seed_add):
    inv = np.float32(1.0 / MOD)
    t = base + c1
    t = jnp.where(t >= MOD, t - MOD, t)
    u = jnp.where(t >= 46337, t - 46337, t)
    p = u * u
    w = (p >> 16) * 32138 - (p & 0xFFFF) * 32802 + (wave_add + c2)
    w = w - (w >> 16) * MOD
    f = w.astype(F32)
    h = f - jnp.floor(f * inv + np.float32(0.5) * inv) * np.float32(MOD)
    u = jnp.where(h >= 46337.0, h - 46337.0, h).astype(jnp.int32)
    p = u * u + seed_add
    v = p - (p >> 16) * MOD
    x = v.astype(F32) * inv + np.float32(0.5 / MOD - 0.5)
    return x - jnp.round(x)


def xor_values(a):
    return [a, a + 1 - 2 * (a % 2), (a + 2) % 4, 3 - a]


def iota(shape, axis):
    return lax.broadcasted_iota(jnp.int32, shape, axis)


def cos_sin(m):
    n = (m + 4096) >> 13
    x = (m - (n << 13)).astype(F32) * np.float32(2.0 * math.pi / 32768)
    y = x * x
    s = x + x * y * (-1.0 / 6 + y * (1.0 / 120 + y * (-1.0 / 5040 + y * np.float32(1.0 / 362880))))
    c = 1.0 + y * (-0.5 + y * (1.0 / 24 + y * (-1.0 / 720 + y * np.float32(1.0 / 40320))))
    n = n & 3
    swap = (n & 1) == 1
    cos, sin = jnp.where(swap, s, c), jnp.where(swap, c, s)
    cos = jnp.where((n == 1) | (n == 2), -cos, cos)
    return cos, jnp.where(n >= 2, -sin, sin)


def wave_tables(i, base, wave_add, wave_sq, twist):
    rows = pl.ds(pl.multiple_of(i * 16, 16), 16)
    k1, k2 = iota((16, DEPTH), 0) + i * 16, iota((16, DEPTH), 1)
    k = k1 + N * k2
    h = k * 7919
    h = h - (h >> 16) * MOD
    base[rows] = jnp.where(h >= MOD, h - MOD, h)
    h = k - (k >> 13) * 8191
    h = jnp.where(h >= 8191, h - 8191, h)
    wave_add[rows] = h * 13 + 16000 * MOD
    ky = jnp.minimum(k, NY - k).astype(F32) * np.float32(1.0 / KAPPA)
    wave_sq[rows] = ky * ky + 1.0
    twist[0, rows], twist[1, rows] = cos_sin(k1 * k2)


def inner_rows(i, inner):
    at = pl.multiple_of(i * 16, 16)
    c, s = cos_sin(((iota((16, DEPTH), 0) + at) * iota((16, DEPTH), 1) & (DEPTH - 1)) * (NY // DEPTH))
    for x, down, right in ((c, 0, 0), (s, 0, 1), (-s, 1, 0), (c, 1, 1)):
        hi, lo = split(x)
        rows, cols = pl.ds(DEPTH * down + at, 16), pl.ds(DEPTH * right, DEPTH)
        inner[0, rows, cols] = hi
        inner[1, rows, cols] = lo


def synth(
    offset, seeds, out,
    base, wave_add, wave_sq, seed_add, twist, inner, outer, amp, xhi, xlo, ybuf, zbuf,
    seed_row, seed_all, par, parf, rows_out, sent, gsend, grecv, ssem, rsem,
):
    me = lax.axis_index("rows")
    mx, mz, my, mc = me // 32, me // 8 % 4, me // 2 % 4, me % 2
    mxz, myc = me // 8, me % 8
    barrier = pltpu.get_barrier_semaphore()
    across = [(mxz + i) % 16 * 8 + myc for i in range(1, 16)]
    along = [mxz * 8 + (myc + i) % 8 for i in range(1, 8)]
    for peer in across + along:
        pl.semaphore_signal(barrier, inc=1, device_id=(peer,), device_id_type=MESH)

    lane = iota((8, N), 1)
    odd, half = lane % 2, lane // 2 % 2
    seed_row[...] = jnp.where(
        half == 0, jnp.where(odd == 0, seeds[0], seeds[2]), jnp.where(odd == 0, seeds[1], seeds[3])
    )

    upper = mx // 2
    flip = lambda a: (a + 2 * upper) % 4
    pair = (mx % 2) * 32 + flip(mz) * 8 + flip(my) * 2 + mc

    def prepare(i, _):
        wave_tables(i, base, wave_add, wave_sq, twist)
        return 0

    def exchange_seeds():
        pl.semaphore_wait(barrier, 22)
        pltpu.make_async_copy(seed_row.at[0], seed_all.at[myc, mxz], grecv.at[0]).start()
        for peer in across:
            pltpu.make_async_remote_copy(
                src_ref=seed_row.at[0],
                dst_ref=seed_all.at[myc, mxz],
                send_sem=gsend.at[0],
                recv_sem=grecv.at[0],
                device_id=(peer,),
                device_id_type=MESH,
            ).start()

    def forward_seeds():
        pltpu.make_async_copy(seed_all.at[0], seed_all.at[0], grecv.at[0]).wait()
        for peer in along:
            pltpu.make_async_remote_copy(
                src_ref=seed_all.at[myc],
                dst_ref=seed_all.at[myc],
                send_sem=gsend.at[1],
                recv_sem=grecv.at[1],
                device_id=(peer,),
                device_id_type=MESH,
            ).start()

    lax.fori_loop(0, N // 16, prepare, 0)
    exchange_seeds()

    for j in range(COLS):
        g = offset[0] + (j * PAIRS + pair)
        c = g * 30011 % MOD
        d = g % 4099 * 7
        par[j, 0] = (c + 17) % MOD
        par[j, 1] = (c + 29011) % MOD
        par[j, 2] = (d + 17) * 32719 % MOD
        par[j, 3] = (d + 29011) * 32719 % MOD
        kx = jnp.minimum(g, NXG - g).astype(F32) * np.float32(1.0 / KAPPA)
        parf[j] = kx * kx

    for at in range(0, PAIRS, 8):
        dest = jnp.concatenate([jnp.full((1, N), m, jnp.int32) for m in MASKS[at : at + 8]], axis=0)
        dest = lax.bitwise_xor(dest, me)
        c, s = cos_sin((dest * iota((8, N), 1) & (N - 1)) * (NY // N))
        for x, i, k in ((c, 0, 0), (-s, 0, 1), (s, 1, 0), (c, 1, 1)):
            ybuf[pl.ds(PAIRS * i + at, 8), pl.ds(N * k, N)] = x
    hi, lo = split(ybuf[: 2 * PAIRS, : 2 * N])
    outer[0] = hi
    outer[1] = lo

    def prepare_inner(i, _):
        inner_rows(i, inner)
        return 0

    forward_seeds()
    lax.fori_loop(0, DEPTH // 16, prepare_inner, 0)

    scale = np.float32(2.0 * 3.4641016151377544 / math.sqrt(NY))

    def amplitude(i, _):
        rows = pl.ds(pl.multiple_of(i * 16, 16), 16)
        z0 = wave_sq[rows]
        for j in range(COLS):
            y = lax.rsqrt(z0 + parf[j])
            amp[j, rows] = y * y * lax.rsqrt(y) * scale
        return 0

    lax.fori_loop(0, N // 16, amplitude, 0)

    pltpu.make_async_copy(seed_all.at[pl.ds(0, 7)], seed_all.at[pl.ds(0, 7)], grecv.at[1]).wait()

    got = seed_all[...].reshape(N, N)
    turned = pltpu.roll(got, 2, 1)
    lane, row = iota((N, N), 1), iota((N, N), 0)
    owner = row % 16 * 8 + row // 16
    for h in range(2):
        picked = jnp.where(lane // 2 % 2 == h, got, turned)
        for t in range(2):
            s = jnp.where(lane // 2 + 64 * t == owner, picked, 0).astype(F32)
            s = jnp.sum(s, axis=0, keepdims=True).astype(jnp.int32)
            rows, cols = pl.ds(64 * h, 64), pl.ds(128 * t, 128)
            a = base[rows, cols] + jnp.broadcast_to(mod_small(s, MOD), (64, 128))
            base[rows, cols] = jnp.where(a >= MOD, a - MOD, a)
            seed_add[rows, cols] = jnp.broadcast_to(mod_small(s, 32749), (64, 128))

    xs, zs = [v * 32 for v in xor_values(mx)], [v * 8 for v in xor_values(mz)]
    ys, cs = [v * 2 for v in xor_values(my)], [mc, 1 - mc]
    dot = lambda a, b: jnp.dot(a, b, preferred_element_type=F32)

    def chunk(ch, _):
        for jj in range(NC):
            j = ch * NC + jj

            def block(i, _):
                at = pl.multiple_of(i * 16, 16)
                rows = pl.ds(at, 16)
                b, w, s, a = base[rows], wave_add[rows], seed_add[rows], amp[j, rows]
                for part in range(2):
                    hi, lo = split(a * noise(b, par[j, part], par[j, 2 + part], w, s))
                    to = pl.ds(jj * N + at, 16)
                    xhi[to, part * DEPTH : (part + 1) * DEPTH] = hi
                    xlo[to, part * DEPTH : (part + 1) * DEPTH] = lo
                return 0

            lax.fori_loop(0, N // 16, block, 0, unroll=2)
        ybuf[...] = dot(xhi[...], inner[0]) + dot(xlo[...], inner[0]) + dot(xhi[...], inner[1])
        for jj in range(NC):
            yr, yi = ybuf[jj * N : (jj + 1) * N, :DEPTH], ybuf[jj * N : (jj + 1) * N, DEPTH:]
            tc, ts = twist[0], twist[1]
            hi, lo = split(jnp.concatenate([yr * tc - yi * ts, yr * ts + yi * tc], axis=0))
            z = dot(outer[0], hi) + dot(outer[0], lo) + dot(outer[1], hi)
            q = (ch * NC + jj) * 2
            zbuf[q] = z[:PAIRS]
            zbuf[q + 1] = z[PAIRS:]
        qs = pl.ds(ch * (2 * NC), 2 * NC)
        for t, (a, b, c, d) in enumerate(NEAR):
            if (a, b, c, d) == (0, 0, 0, 0):
                pltpu.make_async_copy(zbuf.at[qs, t], out.at[qs, pair], rsem.at[ch]).start()
            else:
                pltpu.make_async_remote_copy(
                    src_ref=zbuf.at[qs, t],
                    dst_ref=out.at[qs, pair],
                    send_sem=ssem.at[ch],
                    recv_sem=rsem.at[ch],
                    device_id=(xs[a] + zs[b] + ys[c] + cs[d],),
                    device_id_type=MESH,
                ).start()
        return 0

    lax.fori_loop(0, CHUNKS, chunk, 0)

    pltpu.make_async_copy(rows_out, rows_out, gsend.at[0]).wait()
    pltpu.make_async_copy(seed_all.at[pl.ds(0, 7)], seed_all.at[pl.ds(0, 7)], gsend.at[1]).wait()
    for ch in range(CHUNKS):
        qs = pl.ds(ch * 2 * NC, 2 * NC)
        pltpu.make_async_copy(out.at[qs], out.at[qs], rsem.at[ch]).wait()
        pltpu.make_async_copy(sent, sent, ssem.at[ch]).wait()


def turn(blocks, real, imag, turned, sems):
    eye = (iota((DEPTH, DEPTH), 0) == iota((DEPTH, DEPTH), 1)).astype(F32).astype(BF16)
    dot = lambda x: lax.dot_general(eye, x, (((1,), (1,)), ((), ())), preferred_element_type=F32)
    copies = []
    for i in range(STRIP // 256):
        for part, to in ((0, real), (1, imag)):
            rows = jnp.concatenate([blocks[8 * i + 2 * j + part] for j in range(4)], axis=0)
            hi, lo = split(rows)
            cols = pl.ds(256 * i, 256)
            turned[part, :, cols] = dot(hi) + dot(lo)
            copies.append(pltpu.make_async_copy(turned.at[part, :, cols], to.at[:, cols], sems.at[i, part]))
            copies[-1].start()
    for copy in copies:
        copy.wait()


def shards(seeds, offset):
    scalar = pl.BlockSpec(memory_space=pltpu.SMEM)
    hbm = pl.BlockSpec(memory_space=pltpu.HBM)
    dma = pltpu.SemaphoreType.DMA
    vmem = pltpu.VMEM
    blocks = pl.pallas_call(
        synth,
        out_shape=jax.ShapeDtypeStruct((Q, PAIRS, DEPTH), F32),
        in_specs=[scalar, scalar],
        out_specs=pl.BlockSpec(memory_space=pl.ANY),
        scratch_shapes=[
            vmem((N, DEPTH), jnp.int32),
            vmem((N, DEPTH), jnp.int32),
            vmem((N, DEPTH), F32),
            vmem((N, DEPTH), jnp.int32),
            vmem((2, N, DEPTH), F32),
            vmem((2, 2 * DEPTH, 2 * DEPTH), BF16),
            vmem((2, 2 * PAIRS, 2 * N), BF16),
            vmem((COLS, N, DEPTH), F32),
            vmem((NC * N, 2 * DEPTH), BF16),
            vmem((NC * N, 2 * DEPTH), BF16),
            vmem((NC * N, 2 * DEPTH), F32),
            vmem((Q, PAIRS, DEPTH), F32),
            vmem((8, N), jnp.int32),
            vmem((8, 16, N), jnp.int32),
            pltpu.SMEM((COLS, 4), jnp.int32),
            pltpu.SMEM((COLS,), F32),
            vmem((15, 1, N), jnp.int32),
            vmem((PAIRS - 1, 2 * NC, 1, DEPTH), F32),
            dma((2,)),
            dma((2,)),
            dma((CHUNKS,)),
            dma((CHUNKS,)),
        ],
        compiler_params=pltpu.CompilerParams(
            collective_id=0, has_side_effects=True, vmem_limit_bytes=48 * 2**20
        ),
    )(offset, seeds)
    return pl.pallas_call(
        turn,
        out_shape=[jax.ShapeDtypeStruct((DEPTH, STRIP), F32)] * 2,
        in_specs=[pl.BlockSpec(memory_space=pltpu.VMEM)],
        out_specs=[hbm, hbm],
        scratch_shapes=[vmem((2, DEPTH, STRIP), F32), dma((STRIP // 256, 2))],
        compiler_params=pltpu.CompilerParams(vmem_limit_bytes=16 * 2**20),
    )(blocks)


def solution(mesh):
    in_specs = (P("rows"), P())
    out_specs = (P("rows", None), P("rows", None))
    return jax.shard_map(shards, mesh=mesh, in_specs=in_specs, out_specs=out_specs, check_vma=False)
```

```python
import itertools
import math
import random

import jax
import jax.numpy as jnp
import numpy as np
from jax import lax
from jax.experimental import pallas as pl
from jax.experimental.pallas import tpu as pltpu
from jax.sharding import PartitionSpec as P

NY = 32768
NXG = 65536
STRIP = 1024
KAPPA = 8192
N = 128
DEPTH = 256
PAIRS = 64
COLS = STRIP // PAIRS
SIZES = (2, 2, 3, 4, 5)
STARTS = tuple(sum(SIZES[:i]) for i in range(len(SIZES)))
NC = max(SIZES)
Q = 2 * COLS
MOD = 65521
MESH = pl.DeviceIdType.MESH
F32 = jnp.float32
BF16 = jnp.bfloat16


def hops(offset):
    return sum((0, 1, 2, 1)[a] for a in offset[:3])


def is_near(offset):
    if hops(offset) != 3:
        return hops(offset) < 3
    if 2 not in offset[:3]:
        return sum(a == 3 for a in offset[:3]) % 2 == 0
    return (offset.index(0) + 1) % 3 == offset[:3].index(2)


def near_offsets():
    every = itertools.product(range(4), range(4), range(4), range(2))
    near = [offset for offset in every if is_near(offset)]
    random.Random(3).shuffle(near)
    near.sort(key=hops, reverse=True)
    return near


NEAR = near_offsets()


OTHERS = list(itertools.product(range(4), range(4), range(4), range(2)))[1:]
FAR_FIRST = sorted(OTHERS, key=hops, reverse=True)
MASKS = [((a * 4 + b) * 4 + c) * 2 + d for a, b, c, d in NEAR]


def split(x):
    hi = x.astype(BF16)
    return hi, (x - hi.astype(F32)).astype(BF16)


def mod_small(s, m):
    q = (s.astype(F32) * np.float32(1.0 / m)).astype(jnp.int32)
    r = s - q * m
    r = jnp.where(r < 0, r + m, r)
    return jnp.where(r >= m, r - m, r)


def noise(base, c, wave_add, seed_add):
    low, high, add0, add1, add2, mix = c
    u = base + jnp.where(base < high, jnp.where(base < low, add0, add1), add2)
    p = u * u
    w = p * 32719 + (p >> 15) * (16069 - 32719 * 32768) + (wave_add + mix)
    w = w - (w >> 16) * MOD
    w = w - (w >> 16) * MOD
    u = w - jnp.where(w < 46337, 0, jnp.where(w < MOD, 46337, MOD))
    p = u * u
    return (p * 65551 + (p >> 16) * 225 + seed_add).astype(F32)


def xor_values(a):
    return [a, a + 1 - 2 * (a % 2), (a + 2) % 4, 3 - a]


def iota(shape, axis):
    return lax.broadcasted_iota(jnp.int32, shape, axis)


def cos_sin(m):
    n = (m + 4096) >> 13
    x = (m - (n << 13)).astype(F32) * np.float32(2.0 * math.pi / 32768)
    y = x * x
    s = x + x * y * (-1.0 / 6 + y * (1.0 / 120 + y * (-1.0 / 5040 + y * np.float32(1.0 / 362880))))
    c = 1.0 + y * (-0.5 + y * (1.0 / 24 + y * (-1.0 / 720 + y * np.float32(1.0 / 40320))))
    n = n & 3
    swap = (n & 1) == 1
    cos, sin = jnp.where(swap, s, c), jnp.where(swap, c, s)
    cos = jnp.where((n == 1) | (n == 2), -cos, cos)
    return cos, jnp.where(n >= 2, -sin, sin)


def lane_row(lane):
    return (lane & (N - 1)) * 2 + (lane >> 7)


def wave_tables(i, base, wave_add, wave_sq, twist):
    rows = pl.ds(pl.multiple_of(i * 16, 16), 16)
    k1, k2 = iota((16, DEPTH), 0) + i * 16, iota((16, DEPTH), 1)
    k = k1 + N * k2
    h = k * 7919
    h = h - (h >> 16) * MOD
    base[rows] = jnp.where(h >= MOD, h - MOD, h)
    h = k - (k >> 13) * 8191
    h = jnp.where(h >= 8191, h - 8191, h)
    wave_add[rows] = h * 13
    ky = jnp.minimum(k, NY - k).astype(F32) * np.float32(1.0 / KAPPA)
    wave_sq[rows] = ky * ky + 1.0
    twist[0, rows], twist[1, rows] = cos_sin(k1 * lane_row(k2))


def inner_rows(i, inner):
    at = pl.multiple_of(i * 16, 16)
    row = lane_row(iota((16, DEPTH), 1))
    c, s = cos_sin(((iota((16, DEPTH), 0) + at) * row & (DEPTH - 1)) * (NY // DEPTH))
    for x, down, right in ((c, 0, 0), (s, 0, 1), (-s, 1, 0), (c, 1, 1)):
        hi, lo = split(x)
        cols = pl.ds(N * right, N)
        for part, y in enumerate((hi, hi, lo)):
            rows = pl.ds(DEPTH * part + N * down + at, 16)
            inner[0, rows, cols] = y[:, :N]
            inner[1, rows, cols] = y[:, N:]


def synth(
    offset, seeds_hbm, out,
    base, wave_add, wave_sq, seed_add, twist, inner, outer, amp, xhi, xlo, ybuf, zbuf,
    seed_row, seed_all, par, parf, rows_out, sent, seeds, seeds_sem, gsend, grecv, ssem, rsem,
):
    me = lax.axis_index("rows")
    mx, mz, my, mc = me // 32, me // 8 % 4, me // 2 % 4, me % 2
    xs, zs = [v * 32 for v in xor_values(mx)], [v * 8 for v in xor_values(mz)]
    ys, cs = [v * 2 for v in xor_values(my)], [mc, 1 - mc]
    device = lambda offset: (xs[offset[0]] + zs[offset[1]] + ys[offset[2]] + cs[offset[3]],)
    own = pltpu.make_async_copy(seeds_hbm, seeds, seeds_sem)
    own.start()
    barrier = pltpu.get_barrier_semaphore()
    for to in FAR_FIRST:
        pl.semaphore_signal(barrier, inc=1, device_id=device(to), device_id_type=MESH)

    own.wait()
    lane = iota((8, N), 1)
    odd, half = lane % 2, lane // 2 % 2
    seed_row[...] = jnp.where(
        half == 0, jnp.where(odd == 0, seeds[0], seeds[2]), jnp.where(odd == 0, seeds[1], seeds[3])
    )

    upper = mx // 2
    flip = lambda a: (a + 2 * upper) % 4
    pair = (mx % 2) * 32 + flip(mz) * 8 + flip(my) * 2 + mc

    def prepare(i, _):
        wave_tables(i, base, wave_add, wave_sq, twist)
        return 0

    pl.semaphore_wait(barrier, N - 1)
    pltpu.make_async_copy(seed_row.at[0], seed_all.at[me], grecv).start()
    for to in FAR_FIRST:
        pltpu.make_async_remote_copy(
            src_ref=seed_row.at[0],
            dst_ref=seed_all.at[me],
            send_sem=gsend,
            recv_sem=grecv,
            device_id=device(to),
            device_id_type=MESH,
        ).start()

    lax.fori_loop(0, N // 16, prepare, 0)

    for j in range(COLS):
        g = offset[0] + (j * PAIRS + pair)
        hashed, mixed = g * 30011 % MOD, g % 4099 * 7
        for part, salt in enumerate((17, 29011)):
            c = (hashed + salt) % MOD
            below = c < 46337
            low, high = jnp.where(below, 46337 - c, MOD - c), jnp.where(below, MOD - c, MOD + 46337 - c)
            add0 = jnp.where(below, c, c - 46337)
            add1 = jnp.where(below, c - 46337, c - MOD)
            add2 = jnp.where(below, c - MOD, c - MOD - 46337)
            for i, x in enumerate((low, high, add0, add1, add2, (mixed + salt) * 32719 % MOD)):
                par[j, 6 * part + i] = x
        kx = jnp.minimum(g, NXG - g).astype(F32) * np.float32(1.0 / KAPPA)
        parf[j] = kx * kx

    for at in range(0, PAIRS, 8):
        dest = jnp.concatenate([jnp.full((1, N), m, jnp.int32) for m in MASKS[at : at + 8]], axis=0)
        dest = lax.bitwise_xor(dest, me)
        c, s = cos_sin((dest * iota((8, N), 1) & (N - 1)) * (NY // N))
        for x, i, k in ((c, 0, 0), (-s, 0, 1), (s, 1, 0), (c, 1, 1)):
            ybuf[pl.ds(PAIRS * i + at, 8), pl.ds(N * k, N)] = x
    hi, lo = split(ybuf[: 2 * PAIRS, : 2 * N])
    for part, x in enumerate((hi, hi, lo)):
        outer[:, 2 * N * part : 2 * N * (part + 1)] = x

    def prepare_inner(i, _):
        inner_rows(i, inner)
        return 0

    lax.fori_loop(0, N // 16, prepare_inner, 0)

    scale = np.float32(2.0 * 3.4641016151377544 / math.sqrt(NY) / 2.0**32)

    def amplitude(i, _):
        rows = pl.ds(pl.multiple_of(i * 16, 16), 16)
        z0 = wave_sq[rows]
        for j in range(COLS):
            y = lax.rsqrt(z0 + parf[j])
            amp[j, rows] = y * y * lax.rsqrt(y) * scale
        return 0

    lax.fori_loop(0, N // 16, amplitude, 0)

    pltpu.make_async_copy(seed_all, seed_all, grecv).wait()

    got = seed_all[...]
    turned = pltpu.roll(got, 2, 1)
    lane, row = iota((N, N), 1), iota((N, N), 0)
    for h in range(2):
        picked = jnp.where(lane // 2 % 2 == h, got, turned)
        for t in range(2):
            s = jnp.where(lane // 2 + 64 * t == row, picked, 0).astype(F32)
            s = jnp.sum(s, axis=0, keepdims=True).astype(jnp.int32)
            rows, cols = pl.ds(64 * h, 64), pl.ds(128 * t, 128)
            a = base[rows, cols] + jnp.broadcast_to(mod_small(s, MOD), (64, 128))
            base[rows, cols] = jnp.where(a >= MOD, a - MOD, a)
            seed_add[rows, cols] = jnp.broadcast_to(mod_small(s, 32749) * 65551 + (32776 + 128 - 2**31), (64, 128))

    dot = lambda a, b: jnp.dot(a, b, preferred_element_type=F32)

    def chunk(ch, start, size):
        for jj in range(size):
            j = start + jj

            def block(i, _):
                at = pl.multiple_of(i * 16, 16)
                rows = pl.ds(at, 16)
                b, w, s, a = base[rows], wave_add[rows], seed_add[rows], amp[j, rows]
                into = pl.ds(jj * N + at, 16)
                for part in range(2):
                    f = a * noise(b, [par[j, 6 * part + i] for i in range(6)], w, s)
                    even, odd = f[:, :N] + f[:, N:], f[:, :N] - f[:, N:]
                    for parity, x in enumerate((even, odd)):
                        cols = pl.ds(DEPTH * parity + N * part, N)
                        xhi[into, cols], xlo[into, cols] = split(x)
                return 0

            lax.fori_loop(0, N // 16, block, 0, unroll=8)
        for parity in range(2):
            cols = pl.ds(DEPTH * parity, DEPTH)
            high, low = xhi[: size * N, cols], xlo[: size * N, cols]
            ybuf[: size * N, cols] = dot(jnp.concatenate([high, low, high], axis=1), inner[parity])
        for jj in range(size):
            rows = pl.ds(jj * N, N)
            yr = jnp.concatenate([ybuf[rows, 0 * N : 1 * N], ybuf[rows, 2 * N : 3 * N]], axis=1)
            yi = jnp.concatenate([ybuf[rows, 1 * N : 2 * N], ybuf[rows, 3 * N : 4 * N]], axis=1)
            tc, ts = twist[0], twist[1]
            hi, lo = split(jnp.concatenate([yr * tc - yi * ts, yr * ts + yi * tc], axis=0))
            z = dot(outer[...], jnp.concatenate([hi, lo, hi], axis=0))
            q = (start + jj) * 2
            zbuf[q] = z[:PAIRS]
            zbuf[q + 1] = z[PAIRS:]
        qs = pl.ds(2 * start, 2 * size)
        for t, to in enumerate(NEAR):
            if to == (0, 0, 0, 0):
                pltpu.make_async_copy(zbuf.at[qs, t], out.at[qs, pair], rsem.at[ch]).start()
            else:
                pltpu.make_async_remote_copy(
                    src_ref=zbuf.at[qs, t],
                    dst_ref=out.at[qs, pair],
                    send_sem=ssem.at[ch],
                    recv_sem=rsem.at[ch],
                    device_id=device(to),
                    device_id_type=MESH,
                ).start()

    for ch, (start, size) in enumerate(zip(STARTS, SIZES)):
        chunk(ch, start, size)

    pltpu.make_async_copy(rows_out, rows_out, gsend).wait()
    for ch, (start, size) in enumerate(zip(STARTS, SIZES)):
        qs = pl.ds(2 * start, 2 * size)
        pltpu.make_async_copy(out.at[qs], out.at[qs], rsem.at[ch]).wait()
        gone = sent.at[:, pl.ds(0, 2 * size)]
        pltpu.make_async_copy(gone, gone, ssem.at[ch]).wait()


def turn(blocks, real, imag, turned, sems):
    order = (iota((DEPTH, DEPTH), 0) == lane_row(iota((DEPTH, DEPTH), 1))).astype(F32).astype(BF16)
    dot = lambda x: lax.dot_general(order, x, (((1,), (1,)), ((), ())), preferred_element_type=F32)
    copies = []
    for i in range(STRIP // 256):
        for part, to in ((0, real), (1, imag)):
            rows = jnp.concatenate([blocks[8 * i + 2 * j + part] for j in range(4)], axis=0)
            hi, lo = split(rows)
            cols = pl.ds(256 * i, 256)
            turned[part, :, cols] = dot(hi) + dot(lo)
            copies.append(pltpu.make_async_copy(turned.at[part, :, cols], to.at[:, cols], sems.at[i, part]))
            copies[-1].start()
    for copy in copies:
        copy.wait()


def shards(seeds, offset):
    scalar = pl.BlockSpec(memory_space=pltpu.SMEM)
    hbm = pl.BlockSpec(memory_space=pltpu.HBM)
    dma = pltpu.SemaphoreType.DMA
    vmem = pltpu.VMEM
    blocks = pl.pallas_call(
        synth,
        out_shape=jax.ShapeDtypeStruct((Q, PAIRS, DEPTH), F32),
        in_specs=[scalar, hbm],
        out_specs=pl.BlockSpec(memory_space=pl.ANY),
        scratch_shapes=[
            vmem((N, DEPTH), jnp.int32),
            vmem((N, DEPTH), jnp.int32),
            vmem((N, DEPTH), F32),
            vmem((N, DEPTH), jnp.int32),
            vmem((2, N, DEPTH), F32),
            vmem((2, 3 * DEPTH, DEPTH), BF16),
            vmem((2 * PAIRS, 3 * 2 * N), BF16),
            vmem((COLS, N, DEPTH), F32),
            vmem((NC * N, 2 * DEPTH), BF16),
            vmem((NC * N, 2 * DEPTH), BF16),
            vmem((NC * N, 2 * DEPTH), F32),
            vmem((Q, PAIRS, DEPTH), F32),
            vmem((8, N), jnp.int32),
            vmem((N, N), jnp.int32),
            pltpu.SMEM((COLS, 12), jnp.int32),
            pltpu.SMEM((COLS,), F32),
            vmem((N - 1, 1, N), jnp.int32),
            vmem((PAIRS - 1, 2 * NC, 1, DEPTH), F32),
            pltpu.SMEM((4,), jnp.int32),
            dma,
            dma,
            dma,
            dma((len(SIZES),)),
            dma((len(SIZES),)),
        ],
        compiler_params=pltpu.CompilerParams(
            collective_id=0, has_side_effects=True, vmem_limit_bytes=48 * 2**20
        ),
    )(offset, seeds)
    return pl.pallas_call(
        turn,
        out_shape=[jax.ShapeDtypeStruct((DEPTH, STRIP), F32)] * 2,
        in_specs=[pl.BlockSpec(memory_space=pltpu.VMEM)],
        out_specs=[hbm, hbm],
        scratch_shapes=[vmem((2, DEPTH, STRIP), F32), dma((STRIP // 256, 2))],
        compiler_params=pltpu.CompilerParams(vmem_limit_bytes=16 * 2**20),
    )(blocks)


def solution(mesh):
    in_specs = (P("rows"), P())
    out_specs = (P("rows", None), P("rows", None))
    return jax.shard_map(shards, mesh=mesh, in_specs=in_specs, out_specs=out_specs, check_vma=False)
```

```python
import itertools
import math
import random

import jax
import jax.numpy as jnp
import numpy as np
from jax import lax
from jax.experimental import pallas as pl
from jax.experimental.pallas import tpu as pltpu
from jax.sharding import PartitionSpec as P

NY = 32768
NXG = 65536
STRIP = 1024
KAPPA = 8192
N = 128
DEPTH = 256
PAIRS = 64
QUADS = 32
CHUNKS = ((0, 0, 2), (0, 2, 2), (0, 4, 3), (0, 7, 5), (1, 0, 4), (1, 4, 4))
PAIR_COLS = sum(size for kind, _, size in CHUNKS if kind == 0)
QUAD_COLS = sum(size for kind, _, size in CHUNKS if kind == 1)
COLS = PAIR_COLS + QUAD_COLS
NC = max(size for _, _, size in CHUNKS)
MOD = 65521
MESH = pl.DeviceIdType.MESH
F32 = jnp.float32
BF16 = jnp.bfloat16


def hops(offset):
    return sum((0, 1, 2, 1)[a] for a in offset[:3])


def is_near(offset):
    if hops(offset) != 3:
        return hops(offset) < 3
    if 2 not in offset[:3]:
        return sum(a == 3 for a in offset[:3]) % 2 == 0
    return (offset.index(0) + 1) % 3 == offset[:3].index(2)


def near_offsets():
    every = itertools.product(range(4), range(4), range(4), range(2))
    near = [offset for offset in every if is_near(offset)]
    random.Random(3).shuffle(near)
    near.sort(key=hops, reverse=True)
    return near


NEAR = near_offsets()


OTHERS = list(itertools.product(range(4), range(4), range(4), range(2)))[1:]
FAR_FIRST = sorted(OTHERS, key=hops, reverse=True)
NEAR_QUAD = [
    (a, b ^ c, d, e)
    for a, b in ((0, 0), (1, 0), (3, 0), (0, 1))
    for c, d in ((0, 0), (3, 0), (0, 1), (0, 3))
    for e in range(2)
]
random.Random(4).shuffle(NEAR_QUAD)
NEAR_QUAD.sort(key=hops, reverse=True)
SERVED = (NEAR, NEAR_QUAD)
MASKS = [((a * 4 + b) * 4 + c) * 2 + d for served in SERVED for a, b, c, d in served]


def split(x):
    hi = x.astype(BF16)
    return hi, (x - hi.astype(F32)).astype(BF16)


def mod_small(s, m):
    q = (s.astype(F32) * np.float32(1.0 / m)).astype(jnp.int32)
    r = s - q * m
    r = jnp.where(r < 0, r + m, r)
    return jnp.where(r >= m, r - m, r)


def noise(base, c, wave_add, seed_add):
    low, high, add0, add1, add2, mix = c
    u = base + jnp.where(base < high, jnp.where(base < low, add0, add1), add2)
    p = u * u
    w = p * 32719 + (p >> 15) * (16069 - 32719 * 32768) + (wave_add + mix)
    w = w - (w >> 16) * MOD
    w = w - (w >> 16) * MOD
    u = w - jnp.where(w < 46337, 0, jnp.where(w < MOD, 46337, MOD))
    p = u * u
    return (p * 65551 + (p >> 16) * 225 + seed_add).astype(F32)


def xor_values(a):
    return [a, a + 1 - 2 * (a % 2), (a + 2) % 4, 3 - a]


def iota(shape, axis):
    return lax.broadcasted_iota(jnp.int32, shape, axis)


def cos_sin(m):
    n = (m + 4096) >> 13
    x = (m - (n << 13)).astype(F32) * np.float32(2.0 * math.pi / 32768)
    y = x * x
    s = x + x * y * (-1.0 / 6 + y * (1.0 / 120 + y * (-1.0 / 5040 + y * np.float32(1.0 / 362880))))
    c = 1.0 + y * (-0.5 + y * (1.0 / 24 + y * (-1.0 / 720 + y * np.float32(1.0 / 40320))))
    n = n & 3
    swap = (n & 1) == 1
    cos, sin = jnp.where(swap, s, c), jnp.where(swap, c, s)
    cos = jnp.where((n == 1) | (n == 2), -cos, cos)
    return cos, jnp.where(n >= 2, -sin, sin)


def lane_row(lane):
    return (lane & (N - 1)) * 2 + (lane >> 7)


def wave_tables(i, base, wave_add, wave_sq, twist):
    rows = pl.ds(pl.multiple_of(i * 16, 16), 16)
    k1, k2 = iota((16, DEPTH), 0) + i * 16, iota((16, DEPTH), 1)
    k = k1 + N * k2
    h = k * 7919
    h = h - (h >> 16) * MOD
    base[rows] = jnp.where(h >= MOD, h - MOD, h)
    h = k - (k >> 13) * 8191
    h = jnp.where(h >= 8191, h - 8191, h)
    wave_add[rows] = h * 13
    ky = jnp.minimum(k, NY - k).astype(F32) * np.float32(1.0 / KAPPA)
    wave_sq[rows] = ky * ky + 1.0
    twist[0, rows], twist[1, rows] = cos_sin(k1 * lane_row(k2))


def inner_rows(i, inner):
    at = pl.multiple_of(i * 16, 16)
    row = lane_row(iota((16, DEPTH), 1))
    c, s = cos_sin(((iota((16, DEPTH), 0) + at) * row & (DEPTH - 1)) * (NY // DEPTH))
    for x, down, right in ((c, 0, 0), (s, 0, 1), (-s, 1, 0), (c, 1, 1)):
        hi, lo = split(x)
        cols = pl.ds(N * right, N)
        for part, y in enumerate((hi, hi, lo)):
            rows = pl.ds(DEPTH * part + N * down + at, 16)
            inner[0, rows, cols] = y[:, :N]
            inner[1, rows, cols] = y[:, N:]


def synth(
    offset, seeds_hbm, pair_out, quad_out,
    base, wave_add, wave_sq, seed_add, twist, inner, pair_outer, quad_outer, amp, xhi, xlo, ybuf, pair_z, quad_z,
    seed_row, seed_all, par, parf, rows_out, sent, seeds, seeds_sem, gsend, grecv, ssem, rsem,
):
    me = lax.axis_index("rows")
    mx, mz, my, mc = me // 32, me // 8 % 4, me // 2 % 4, me % 2
    xs, zs = [v * 32 for v in xor_values(mx)], [v * 8 for v in xor_values(mz)]
    ys, cs = [v * 2 for v in xor_values(my)], [mc, 1 - mc]
    device = lambda offset: (xs[offset[0]] + zs[offset[1]] + ys[offset[2]] + cs[offset[3]],)
    own = pltpu.make_async_copy(seeds_hbm, seeds, seeds_sem)
    own.start()
    barrier = pltpu.get_barrier_semaphore()
    for to in FAR_FIRST:
        pl.semaphore_signal(barrier, inc=1, device_id=device(to), device_id_type=MESH)

    own.wait()
    lane = iota((8, N), 1)
    odd, half = lane % 2, lane // 2 % 2
    seed_row[...] = jnp.where(
        half == 0, jnp.where(odd == 0, seeds[0], seeds[2]), jnp.where(odd == 0, seeds[1], seeds[3])
    )

    upper = mx // 2
    flip = lambda a: (a + 2 * upper) % 4
    pair = (mx % 2) * 32 + flip(mz) * 8 + flip(my) * 2 + mc

    xg, zg, yg = mx // 2, mz // 2, my // 2
    x0, z0, y0 = (mx + xg) % 2, (mz + zg) % 2, (my + yg) % 2
    quad = (((x0 + xg) % 2 * 2 + (z0 + xg) % 2) * 2 + (zg + yg) % 2) * 2 + (y0 + yg) % 2
    quad = quad * 2 + mc
    kinds = (
        (NEAR, pair, pair_outer, pair_z, pair_out),
        (NEAR_QUAD, quad, quad_outer, quad_z, quad_out),
    )

    def prepare(i, _):
        wave_tables(i, base, wave_add, wave_sq, twist)
        return 0

    pl.semaphore_wait(barrier, N - 1)
    pltpu.make_async_copy(seed_row.at[0], seed_all.at[me], grecv).start()
    for to in FAR_FIRST:
        pltpu.make_async_remote_copy(
            src_ref=seed_row.at[0],
            dst_ref=seed_all.at[me],
            send_sem=gsend,
            recv_sem=grecv,
            device_id=device(to),
            device_id_type=MESH,
        ).start()

    lax.fori_loop(0, N // 16, prepare, 0)

    for j in range(COLS):
        if j < PAIR_COLS:
            g = offset[0] + (j * PAIRS + pair)
        else:
            g = offset[0] + (PAIR_COLS * PAIRS + (j - PAIR_COLS) * QUADS + quad)
        hashed, mixed = g * 30011 % MOD, g % 4099 * 7
        for part, salt in enumerate((17, 29011)):
            c = (hashed + salt) % MOD
            below = c < 46337
            low, high = jnp.where(below, 46337 - c, MOD - c), jnp.where(below, MOD - c, MOD + 46337 - c)
            add0 = jnp.where(below, c, c - 46337)
            add1 = jnp.where(below, c - 46337, c - MOD)
            add2 = jnp.where(below, c - MOD, c - MOD - 46337)
            for i, x in enumerate((low, high, add0, add1, add2, (mixed + salt) * 32719 % MOD)):
                par[j, 6 * part + i] = x
        kx = jnp.minimum(g, NXG - g).astype(F32) * np.float32(1.0 / KAPPA)
        parf[j] = kx * kx

    for at in range(0, PAIRS + QUADS, 8):
        dest = jnp.concatenate([jnp.full((1, N), m, jnp.int32) for m in MASKS[at : at + 8]], axis=0)
        dest = lax.bitwise_xor(dest, me)
        c, s = cos_sin((dest * iota((8, N), 1) & (N - 1)) * (NY // N))
        first, count = (0, PAIRS) if at < PAIRS else (PAIRS, QUADS)
        for x, i, k in ((c, 0, 0), (-s, 0, 1), (s, 1, 0), (c, 1, 1)):
            ybuf[pl.ds(first + count * i + at, 8), pl.ds(N * k, N)] = x
    for outer, first in ((pair_outer, 0), (quad_outer, 2 * PAIRS)):
        hi, lo = split(ybuf[first : first + outer.shape[0], : 2 * N])
        for part, x in enumerate((hi, hi, lo)):
            outer[:, 2 * N * part : 2 * N * (part + 1)] = x

    def prepare_inner(i, _):
        inner_rows(i, inner)
        return 0

    lax.fori_loop(0, N // 16, prepare_inner, 0)

    scale = np.float32(2.0 * 3.4641016151377544 / math.sqrt(NY) / 2.0**32)

    def amplitude(i, _):
        rows = pl.ds(pl.multiple_of(i * 16, 16), 16)
        z0 = wave_sq[rows]
        for j in range(COLS):
            y = lax.rsqrt(z0 + parf[j])
            amp[j, rows] = y * y * lax.rsqrt(y) * scale
        return 0

    lax.fori_loop(0, N // 16, amplitude, 0)

    pltpu.make_async_copy(seed_all, seed_all, grecv).wait()

    got = seed_all[...]
    turned = pltpu.roll(got, 2, 1)
    lane, row = iota((N, N), 1), iota((N, N), 0)
    for h in range(2):
        picked = jnp.where(lane // 2 % 2 == h, got, turned)
        for t in range(2):
            s = jnp.where(lane // 2 + 64 * t == row, picked, 0).astype(F32)
            s = jnp.sum(s, axis=0, keepdims=True).astype(jnp.int32)
            rows, cols = pl.ds(64 * h, 64), pl.ds(128 * t, 128)
            a = base[rows, cols] + jnp.broadcast_to(mod_small(s, MOD), (64, 128))
            base[rows, cols] = jnp.where(a >= MOD, a - MOD, a)
            seed_add[rows, cols] = jnp.broadcast_to(mod_small(s, 32749) * 65551 + (32776 + 128 - 2**31), (64, 128))

    dot = lambda a, b: jnp.dot(a, b, preferred_element_type=F32)

    def chunk(ch, kind, start, size):
        served, group, outer, zbuf, out = kinds[kind]
        count = len(served)
        for jj in range(size):
            j = kind * PAIR_COLS + start + jj

            def block(i, _):
                at = pl.multiple_of(i * 16, 16)
                rows = pl.ds(at, 16)
                b, w, s, a = base[rows], wave_add[rows], seed_add[rows], amp[j, rows]
                into = pl.ds(jj * N + at, 16)
                for part in range(2):
                    f = a * noise(b, [par[j, 6 * part + i] for i in range(6)], w, s)
                    even, odd = f[:, :N] + f[:, N:], f[:, :N] - f[:, N:]
                    for parity, x in enumerate((even, odd)):
                        cols = pl.ds(DEPTH * parity + N * part, N)
                        xhi[into, cols], xlo[into, cols] = split(x)
                return 0

            lax.fori_loop(0, N // 16, block, 0, unroll=8)
        for parity in range(2):
            cols = pl.ds(DEPTH * parity, DEPTH)
            high, low = xhi[: size * N, cols], xlo[: size * N, cols]
            ybuf[: size * N, cols] = dot(jnp.concatenate([high, low, high], axis=1), inner[parity])
        for jj in range(size):
            rows = pl.ds(jj * N, N)
            yr = jnp.concatenate([ybuf[rows, 0 * N : 1 * N], ybuf[rows, 2 * N : 3 * N]], axis=1)
            yi = jnp.concatenate([ybuf[rows, 1 * N : 2 * N], ybuf[rows, 3 * N : 4 * N]], axis=1)
            tc, ts = twist[0], twist[1]
            hi, lo = split(jnp.concatenate([yr * tc - yi * ts, yr * ts + yi * tc], axis=0))
            z = dot(outer[...], jnp.concatenate([hi, lo, hi], axis=0))
            q = (start + jj) * 2
            zbuf[q] = z[:count]
            zbuf[q + 1] = z[count:]
        qs = pl.ds(2 * start, 2 * size)
        for t, to in enumerate(served):
            if to == (0, 0, 0, 0):
                pltpu.make_async_copy(zbuf.at[qs, t], out.at[qs, group], rsem.at[ch]).start()
            else:
                pltpu.make_async_remote_copy(
                    src_ref=zbuf.at[qs, t],
                    dst_ref=out.at[qs, group],
                    send_sem=ssem.at[ch],
                    recv_sem=rsem.at[ch],
                    device_id=device(to),
                    device_id_type=MESH,
                ).start()

    for ch, (kind, start, size) in enumerate(CHUNKS):
        chunk(ch, kind, start, size)

    pltpu.make_async_copy(rows_out, rows_out, gsend).wait()
    for ch, (kind, start, size) in enumerate(CHUNKS):
        served, out = kinds[kind][0], kinds[kind][-1]
        qs = pl.ds(2 * start, 2 * size)
        pltpu.make_async_copy(out.at[qs], out.at[qs], rsem.at[ch]).wait()
        gone = sent.at[pl.ds(0, len(served) - 1), pl.ds(0, 2 * size)]
        pltpu.make_async_copy(gone, gone, ssem.at[ch]).wait()


def turn(pairs, quads, real, imag, turned, sems):
    order = (iota((DEPTH, DEPTH), 0) == lane_row(iota((DEPTH, DEPTH), 1))).astype(F32).astype(BF16)
    dot = lambda x: lax.dot_general(order, x, (((1,), (1,)), ((), ())), preferred_element_type=F32)
    copies = []
    for i in range(STRIP // 256):
        for part, to in ((0, real), (1, imag)):
            if i < PAIR_COLS // 4:
                rows = [pairs[8 * i + 2 * j + part] for j in range(4)]
            else:
                rows = [quads[16 * (i - PAIR_COLS // 4) + 2 * j + part] for j in range(8)]
            rows = jnp.concatenate(rows, axis=0)
            hi, lo = split(rows)
            cols = pl.ds(256 * i, 256)
            turned[part, :, cols] = dot(hi) + dot(lo)
            copies.append(pltpu.make_async_copy(turned.at[part, :, cols], to.at[:, cols], sems.at[i, part]))
            copies[-1].start()
    for copy in copies:
        copy.wait()


def shards(seeds, offset):
    scalar = pl.BlockSpec(memory_space=pltpu.SMEM)
    hbm = pl.BlockSpec(memory_space=pltpu.HBM)
    dma = pltpu.SemaphoreType.DMA
    vmem = pltpu.VMEM
    pairs, quads = pl.pallas_call(
        synth,
        out_shape=[
            jax.ShapeDtypeStruct((2 * PAIR_COLS, PAIRS, DEPTH), F32),
            jax.ShapeDtypeStruct((2 * QUAD_COLS, QUADS, DEPTH), F32),
        ],
        in_specs=[scalar, hbm],
        out_specs=[pl.BlockSpec(memory_space=pl.ANY)] * 2,
        scratch_shapes=[
            vmem((N, DEPTH), jnp.int32),
            vmem((N, DEPTH), jnp.int32),
            vmem((N, DEPTH), F32),
            vmem((N, DEPTH), jnp.int32),
            vmem((2, N, DEPTH), F32),
            vmem((2, 3 * DEPTH, DEPTH), BF16),
            vmem((2 * PAIRS, 3 * 2 * N), BF16),
            vmem((2 * QUADS, 3 * 2 * N), BF16),
            vmem((COLS, N, DEPTH), F32),
            vmem((NC * N, 2 * DEPTH), BF16),
            vmem((NC * N, 2 * DEPTH), BF16),
            vmem((NC * N, 2 * DEPTH), F32),
            vmem((2 * PAIR_COLS, PAIRS, DEPTH), F32),
            vmem((2 * QUAD_COLS, QUADS, DEPTH), F32),
            vmem((8, N), jnp.int32),
            vmem((N, N), jnp.int32),
            pltpu.SMEM((COLS, 12), jnp.int32),
            pltpu.SMEM((COLS,), F32),
            vmem((N - 1, 1, N), jnp.int32),
            vmem((PAIRS - 1, 2 * NC, 1, DEPTH), F32),
            pltpu.SMEM((4,), jnp.int32),
            dma,
            dma,
            dma,
            dma((len(CHUNKS),)),
            dma((len(CHUNKS),)),
        ],
        compiler_params=pltpu.CompilerParams(
            collective_id=0, has_side_effects=True, vmem_limit_bytes=48 * 2**20
        ),
    )(offset, seeds)
    return pl.pallas_call(
        turn,
        out_shape=[jax.ShapeDtypeStruct((DEPTH, STRIP), F32)] * 2,
        in_specs=[pl.BlockSpec(memory_space=pltpu.VMEM)] * 2,
        out_specs=[hbm, hbm],
        scratch_shapes=[vmem((2, DEPTH, STRIP), F32), dma((STRIP // 256, 2))],
        compiler_params=pltpu.CompilerParams(vmem_limit_bytes=16 * 2**20),
    )(pairs, quads)


def solution(mesh):
    in_specs = (P("rows"), P())
    out_specs = (P("rows", None), P("rows", None))
    return jax.shard_map(shards, mesh=mesh, in_specs=in_specs, out_specs=out_specs, check_vma=False)
```

```python
import itertools
import math
import random

import jax
import jax.numpy as jnp
import numpy as np
from jax import lax
from jax.experimental import pallas as pl
from jax.experimental.pallas import tpu as pltpu
from jax.sharding import PartitionSpec as P

NY = 32768
NXG = 65536
STRIP = 1024
KAPPA = 8192
N = 128
DEPTH = 256
PAIRS = 64
QUADS = 32
CHUNKS = ((0, 0, 2), (0, 2, 2), (0, 4, 3), (0, 7, 5), (1, 0, 4), (1, 4, 4))
PAIR_COLS = sum(size for kind, _, size in CHUNKS if kind == 0)
QUAD_COLS = sum(size for kind, _, size in CHUNKS if kind == 1)
COLS = PAIR_COLS + QUAD_COLS
NC = max(size for _, _, size in CHUNKS)
MOD = 65521
MESH = pl.DeviceIdType.MESH
F32 = jnp.float32
BF16 = jnp.bfloat16


def hops(offset):
    return sum((0, 1, 2, 1)[a] for a in offset[:3])


def is_near(offset):
    if hops(offset) != 3:
        return hops(offset) < 3
    if 2 not in offset[:3]:
        return sum(a == 3 for a in offset[:3]) % 2 == 0
    return (offset.index(0) + 1) % 3 == offset[:3].index(2)


def near_offsets():
    every = itertools.product(range(4), range(4), range(4), range(2))
    near = [offset for offset in every if is_near(offset)]
    random.Random(3).shuffle(near)
    near.sort(key=hops, reverse=True)
    return near


NEAR = near_offsets()


OTHERS = list(itertools.product(range(4), range(4), range(4), range(2)))[1:]
FAR_FIRST = sorted(OTHERS, key=hops, reverse=True)
NEAR_QUAD = [
    (a, b ^ c, d, e)
    for a, b in ((0, 0), (1, 0), (3, 0), (0, 1))
    for c, d in ((0, 0), (3, 0), (0, 1), (0, 3))
    for e in range(2)
]
random.Random(4).shuffle(NEAR_QUAD)
NEAR_QUAD.sort(key=hops, reverse=True)
SERVED = (NEAR, NEAR_QUAD)
MASKS = [((a * 4 + b) * 4 + c) * 2 + d for served in SERVED for a, b, c, d in served]


def split(x):
    hi = x.astype(BF16)
    return hi, (x - hi.astype(F32)).astype(BF16)


def mod_small(s, m):
    q = (s.astype(F32) * np.float32(1.0 / m)).astype(jnp.int32)
    r = s - q * m
    r = jnp.where(r < 0, r + m, r)
    return jnp.where(r >= m, r - m, r)


def noise(base, c, wave_add, seed_add):
    low, high, add0, add1, add2, mix = c
    u = base + jnp.where(base < high, jnp.where(base < low, add0, add1), add2)
    p = u * u
    w = p * 32719 + (p >> 15) * (16069 - 32719 * 32768) + (wave_add + mix)
    w = w - (w >> 16) * MOD
    w = w - (w >> 16) * MOD
    u = w - jnp.where(w < 46337, 0, jnp.where(w < MOD, 46337, MOD))
    p = u * u
    return (p * 65551 + (p >> 16) * 225 + seed_add).astype(F32)


def xor_values(a):
    return [a, a + 1 - 2 * (a % 2), (a + 2) % 4, 3 - a]


def iota(shape, axis):
    return lax.broadcasted_iota(jnp.int32, shape, axis)


def cos_sin(m):
    n = (m + 4096) >> 13
    x = (m - (n << 13)).astype(F32) * np.float32(2.0 * math.pi / 32768)
    y = x * x
    s = x + x * y * (-1.0 / 6 + y * (1.0 / 120 + y * (-1.0 / 5040 + y * np.float32(1.0 / 362880))))
    c = 1.0 + y * (-0.5 + y * (1.0 / 24 + y * (-1.0 / 720 + y * np.float32(1.0 / 40320))))
    n = n & 3
    swap = (n & 1) == 1
    cos, sin = jnp.where(swap, s, c), jnp.where(swap, c, s)
    cos = jnp.where((n == 1) | (n == 2), -cos, cos)
    return cos, jnp.where(n >= 2, -sin, sin)


def lane_row(lane):
    return (lane & (N - 1)) * 2 + (lane >> 7)


def wave_tables(i, base, wave_add, wave_sq, twist):
    rows = pl.ds(pl.multiple_of(i * 16, 16), 16)
    k1, k2 = iota((16, DEPTH), 0) + i * 16, iota((16, DEPTH), 1)
    k = k1 + N * k2
    h = k * 7919
    h = h - (h >> 16) * MOD
    base[rows] = jnp.where(h >= MOD, h - MOD, h)
    h = k - (k >> 13) * 8191
    h = jnp.where(h >= 8191, h - 8191, h)
    wave_add[rows] = h * 13
    ky = jnp.minimum(k, NY - k).astype(F32) * np.float32(1.0 / KAPPA)
    wave_sq[rows] = ky * ky + 1.0
    twist[0, rows], twist[1, rows] = cos_sin(k1 * lane_row(k2))


def inner_rows(i, inner):
    at = pl.multiple_of(i * 16, 16)
    row = lane_row(iota((16, DEPTH), 1))
    c, s = cos_sin(((iota((16, DEPTH), 0) + at) * row & (DEPTH - 1)) * (NY // DEPTH))
    for x, down, right in ((c, 0, 0), (s, 0, 1), (-s, 1, 0), (c, 1, 1)):
        hi, lo = split(x)
        cols = pl.ds(N * right, N)
        for part, y in enumerate((hi, hi, lo)):
            rows = pl.ds(DEPTH * part + N * down + at, 16)
            inner[0, rows, cols] = y[:, :N]
            inner[1, rows, cols] = y[:, N:]


def synth(
    offset, seeds_hbm, pair_out, quad_out,
    base, wave_add, wave_sq, seed_add, twist, inner, pair_outer, quad_outer, amp, xhi, xlo, ybuf, pair_z, quad_z,
    seed_row, seed_all, par, parf, rows_out, sent, seeds, seeds_sem, gsend, grecv, ssem, rsem,
):
    me = lax.axis_index("rows")
    mx, mz, my, mc = me // 32, me // 8 % 4, me // 2 % 4, me % 2
    xs, zs = [v * 32 for v in xor_values(mx)], [v * 8 for v in xor_values(mz)]
    ys, cs = [v * 2 for v in xor_values(my)], [mc, 1 - mc]
    device = lambda offset: (xs[offset[0]] + zs[offset[1]] + ys[offset[2]] + cs[offset[3]],)
    own = pltpu.make_async_copy(seeds_hbm, seeds, seeds_sem)
    own.start()
    barrier = pltpu.get_barrier_semaphore()
    for to in FAR_FIRST:
        pl.semaphore_signal(barrier, inc=1, device_id=device(to), device_id_type=MESH)

    own.wait()
    lane = iota((8, N), 1)
    odd, half = lane % 2, lane // 2 % 2
    seed_row[...] = jnp.where(
        half == 0, jnp.where(odd == 0, seeds[0], seeds[2]), jnp.where(odd == 0, seeds[1], seeds[3])
    )

    upper = mx // 2
    flip = lambda a: (a + 2 * upper) % 4
    pair = (mx % 2) * 32 + flip(mz) * 8 + flip(my) * 2 + mc

    xg, zg, yg = mx // 2, mz // 2, my // 2
    x0, z0, y0 = (mx + xg) % 2, (mz + zg) % 2, (my + yg) % 2
    quad = (((x0 + xg) % 2 * 2 + (z0 + xg) % 2) * 2 + (zg + yg) % 2) * 2 + (y0 + yg) % 2
    quad = quad * 2 + mc
    kinds = (
        (NEAR, pair, pair_outer, pair_z, pair_out),
        (NEAR_QUAD, quad, quad_outer, quad_z, quad_out),
    )

    def prepare(i, _):
        wave_tables(i, base, wave_add, wave_sq, twist)
        return 0

    pl.semaphore_wait(barrier, N - 1)
    pltpu.make_async_copy(seed_row.at[0], seed_all.at[me], grecv).start()
    for to in FAR_FIRST:
        pltpu.make_async_remote_copy(
            src_ref=seed_row.at[0],
            dst_ref=seed_all.at[me],
            send_sem=gsend,
            recv_sem=grecv,
            device_id=device(to),
            device_id_type=MESH,
        ).start()

    lax.fori_loop(0, N // 16, prepare, 0)

    for j in range(COLS):
        if j < PAIR_COLS:
            g = offset[0] + (j * PAIRS + pair)
        else:
            g = offset[0] + (PAIR_COLS * PAIRS + (j - PAIR_COLS) * QUADS + quad)
        hashed, mixed = g * 30011 % MOD, g % 4099 * 7
        for part, salt in enumerate((17, 29011)):
            c = (hashed + salt) % MOD
            below = c < 46337
            low, high = jnp.where(below, 46337 - c, MOD - c), jnp.where(below, MOD - c, MOD + 46337 - c)
            add0 = jnp.where(below, c, c - 46337)
            add1 = jnp.where(below, c - 46337, c - MOD)
            add2 = jnp.where(below, c - MOD, c - MOD - 46337)
            for i, x in enumerate((low, high, add0, add1, add2, (mixed + salt) * 32719 % MOD)):
                par[j, 6 * part + i] = x
        kx = jnp.minimum(g, NXG - g).astype(F32) * np.float32(1.0 / KAPPA)
        parf[j] = kx * kx

    for at in range(0, PAIRS + QUADS, 8):
        dest = jnp.concatenate([jnp.full((1, N), m, jnp.int32) for m in MASKS[at : at + 8]], axis=0)
        dest = lax.bitwise_xor(dest, me)
        c, s = cos_sin((dest * iota((8, N), 1) & (N - 1)) * (NY // N))
        first, count = (0, PAIRS) if at < PAIRS else (PAIRS, QUADS)
        for x, i, k in ((c, 0, 0), (-s, 0, 1), (s, 1, 0), (c, 1, 1)):
            ybuf[pl.ds(first + count * i + at, 8), pl.ds(N * k, N)] = x
    for outer, first in ((pair_outer, 0), (quad_outer, 2 * PAIRS)):
        hi, lo = split(ybuf[first : first + outer.shape[0], : 2 * N])
        for part, x in enumerate((hi, hi, lo)):
            outer[:, 2 * N * part : 2 * N * (part + 1)] = x

    def prepare_inner(i, _):
        inner_rows(i, inner)
        return 0

    lax.fori_loop(0, N // 16, prepare_inner, 0)

    scale = np.float32(2.0 * 3.4641016151377544 / math.sqrt(NY) / 2.0**32)

    def amplitude(i, _):
        rows = pl.ds(pl.multiple_of(i * 16, 16), 16)
        z0 = wave_sq[rows]
        for j in range(COLS):
            y = lax.rsqrt(z0 + parf[j])
            amp[j, rows] = y * y * lax.rsqrt(y) * scale
        return 0

    lax.fori_loop(0, N // 16, amplitude, 0)

    pltpu.make_async_copy(seed_all, seed_all, grecv).wait()

    got = seed_all[...]
    turned = pltpu.roll(got, 2, 1)
    lane, row = iota((N, N), 1), iota((N, N), 0)
    for h in range(2):
        picked = jnp.where(lane // 2 % 2 == h, got, turned)
        for t in range(2):
            s = jnp.where(lane // 2 + 64 * t == row, picked, 0).astype(F32)
            s = jnp.sum(s, axis=0, keepdims=True).astype(jnp.int32)
            rows, cols = pl.ds(64 * h, 64), pl.ds(128 * t, 128)
            a = base[rows, cols] + jnp.broadcast_to(mod_small(s, MOD), (64, 128))
            base[rows, cols] = jnp.where(a >= MOD, a - MOD, a)
            seed_add[rows, cols] = jnp.broadcast_to(mod_small(s, 32749) * 65551 + (32776 + 128 - 2**31), (64, 128))

    dot = lambda a, b: jnp.dot(a, b, preferred_element_type=F32)

    def chunk(ch, kind, start, size):
        served, group, outer, zbuf, out = kinds[kind]
        count = len(served)
        for jj in range(size):
            j = kind * PAIR_COLS + start + jj

            def block(i, _):
                at = pl.multiple_of(i * 16, 16)
                rows = pl.ds(at, 16)
                b, w, s, a = base[rows], wave_add[rows], seed_add[rows], amp[j, rows]
                into = pl.ds(jj * N + at, 16)
                for part in range(2):
                    f = a * noise(b, [par[j, 6 * part + i] for i in range(6)], w, s)
                    even, odd = f[:, :N] + f[:, N:], f[:, :N] - f[:, N:]
                    for parity, x in enumerate((even, odd)):
                        cols = pl.ds(DEPTH * parity + N * part, N)
                        xhi[into, cols], xlo[into, cols] = split(x)
                return 0

            lax.fori_loop(0, N // 16, block, 0, unroll=8)
        for parity in range(2):
            cols = pl.ds(DEPTH * parity, DEPTH)
            high, low = xhi[: size * N, cols], xlo[: size * N, cols]
            ybuf[: size * N, cols] = dot(jnp.concatenate([high, low, high], axis=1), inner[parity])
        for jj in range(size):
            rows = pl.ds(jj * N, N)
            yr = jnp.concatenate([ybuf[rows, 0 * N : 1 * N], ybuf[rows, 2 * N : 3 * N]], axis=1)
            yi = jnp.concatenate([ybuf[rows, 1 * N : 2 * N], ybuf[rows, 3 * N : 4 * N]], axis=1)
            tc, ts = twist[0], twist[1]
            hi, lo = split(jnp.concatenate([yr * tc - yi * ts, yr * ts + yi * tc], axis=0))
            z = dot(outer[...], jnp.concatenate([hi, lo, hi], axis=0))
            q = (start + jj) * 2
            zbuf[q] = z[:count]
            zbuf[q + 1] = z[count:]
        qs = pl.ds(2 * start, 2 * size)
        for t, to in enumerate(served):
            if to == (0, 0, 0, 0):
                pltpu.make_async_copy(zbuf.at[qs, t], out.at[qs, group], rsem.at[ch]).start()
            else:
                pltpu.make_async_remote_copy(
                    src_ref=zbuf.at[qs, t],
                    dst_ref=out.at[qs, group],
                    send_sem=ssem.at[ch],
                    recv_sem=rsem.at[ch],
                    device_id=device(to),
                    device_id_type=MESH,
                ).start()

    for ch, (kind, start, size) in enumerate(CHUNKS):
        chunk(ch, kind, start, size)

    pltpu.make_async_copy(rows_out, rows_out, gsend).wait()
    for ch, (kind, start, size) in enumerate(CHUNKS):
        served, out = kinds[kind][0], kinds[kind][-1]
        qs = pl.ds(2 * start, 2 * size)
        pltpu.make_async_copy(out.at[qs], out.at[qs], rsem.at[ch]).wait()
        gone = sent.at[pl.ds(0, len(served) - 1), pl.ds(0, 2 * size)]
        pltpu.make_async_copy(gone, gone, ssem.at[ch]).wait()


def turn(pairs, quads, real, imag, turned, sems):
    order = (iota((DEPTH, DEPTH), 0) == lane_row(iota((DEPTH, DEPTH), 1))).astype(F32).astype(BF16)
    dot = lambda x: lax.dot_general(order, x, (((1,), (1,)), ((), ())), preferred_element_type=F32)
    copies = []
    for i in range(STRIP // 256):
        for part, to in ((0, real), (1, imag)):
            if i < PAIR_COLS // 4:
                rows = [pairs[8 * i + 2 * j + part] for j in range(4)]
            else:
                rows = [quads[16 * (i - PAIR_COLS // 4) + 2 * j + part] for j in range(8)]
            rows = jnp.concatenate(rows, axis=0)
            hi, lo = split(rows)
            cols = pl.ds(256 * i, 256)
            turned[part, :, cols] = dot(hi) + dot(lo)
            copies.append(pltpu.make_async_copy(turned.at[part, :, cols], to.at[:, cols], sems.at[i, part]))
            copies[-1].start()
    for copy in copies:
        copy.wait()


def shards(seeds, offset):
    scalar = pl.BlockSpec(memory_space=pltpu.SMEM)
    hbm = pl.BlockSpec(memory_space=pltpu.HBM)
    dma = pltpu.SemaphoreType.DMA
    vmem = pltpu.VMEM
    pairs, quads = pl.pallas_call(
        synth,
        out_shape=[
            vmem((2 * PAIR_COLS, PAIRS, DEPTH), F32),
            vmem((2 * QUAD_COLS, QUADS, DEPTH), F32),
        ],
        in_specs=[scalar, hbm],
        out_specs=[pl.BlockSpec(memory_space=pl.ANY)] * 2,
        scratch_shapes=[
            vmem((N, DEPTH), jnp.int32),
            vmem((N, DEPTH), jnp.int32),
            vmem((N, DEPTH), F32),
            vmem((N, DEPTH), jnp.int32),
            vmem((2, N, DEPTH), F32),
            vmem((2, 3 * DEPTH, DEPTH), BF16),
            vmem((2 * PAIRS, 3 * 2 * N), BF16),
            vmem((2 * QUADS, 3 * 2 * N), BF16),
            vmem((COLS, N, DEPTH), F32),
            vmem((NC * N, 2 * DEPTH), BF16),
            vmem((NC * N, 2 * DEPTH), BF16),
            vmem((NC * N, 2 * DEPTH), F32),
            vmem((2 * PAIR_COLS, PAIRS, DEPTH), F32),
            vmem((2 * QUAD_COLS, QUADS, DEPTH), F32),
            vmem((8, N), jnp.int32),
            vmem((N, N), jnp.int32),
            pltpu.SMEM((COLS, 12), jnp.int32),
            pltpu.SMEM((COLS,), F32),
            vmem((N - 1, 1, N), jnp.int32),
            vmem((PAIRS - 1, 2 * NC, 1, DEPTH), F32),
            pltpu.SMEM((4,), jnp.int32),
            dma,
            dma,
            dma,
            dma((len(CHUNKS),)),
            dma((len(CHUNKS),)),
        ],
        compiler_params=pltpu.CompilerParams(
            collective_id=0, has_side_effects=True, vmem_limit_bytes=52 * 2**20
        ),
    )(offset, seeds)
    return pl.pallas_call(
        turn,
        out_shape=[jax.ShapeDtypeStruct((DEPTH, STRIP), F32)] * 2,
        in_specs=[pl.BlockSpec(memory_space=pltpu.VMEM)] * 2,
        out_specs=[hbm, hbm],
        scratch_shapes=[vmem((2, DEPTH, STRIP), F32), dma((STRIP // 256, 2))],
        compiler_params=pltpu.CompilerParams(vmem_limit_bytes=16 * 2**20),
    )(pairs, quads)


def solution(mesh):
    in_specs = (P("rows"), P())
    out_specs = (P("rows", None), P("rows", None))
    return jax.shard_map(shards, mesh=mesh, in_specs=in_specs, out_specs=out_specs, check_vma=False)
```
